128 devices in a mesh: group: 4 (over x), col: 32 (over y, z, core).
Axes of the slice: x: 4, y: 4, z: 4, core: 2. Of those that a mesh axis runs over, the one named last changes fastest.
Arguments:
- momentum: bfloat16 [4, 14336, 2048], P(None, ('group', 'col')), may hold values from -6 to 6
- lengths: int32 [4, 128], P(None, ('group', 'col')), may hold values from 1 to 112, 7168 in all within a row
- weight: float32 [4, 14336, 2048], P(None, ('group', 'col')), may hold values from -6 to 6
Outputs:
- update: bfloat16 [4, 14336, 2048], P(None, ('group', 'col'))
- new_weight: float32 [4, 14336, 2048], P(None, ('group', 'col'))
The draws below stay inside these ranges and needn't reach their ends.
Inputs may be any that keep to these rules, and one draw needn't show every extreme that they name: For every expert the 128 lengths sum to 7168, and some device's shard of each expert holds exactly 112 live rows.
All inputs are finite; a program needn't handle non-finite values.
Results may differ from the reference program's by a relative error of at most 0.005.
Values may be sent and summed in bfloat16 or wider, within the bound.
No kernel may reach another device: no remote copies, remote signals or barrier semaphores. Data moves between devices by JAX's collectives and lax.ppermute only.
A program may use at most 128 MiB of HBM per device.

```python
import math
import jax
import jax.numpy as jnp
import numpy as np
from jax import lax

R = 2048
C = 7168
EXPERTS = 4
CAP = 112
DEVICES = 128


def shard_levels(stream_key, extent, cuts, least, top_value):
    level = 1.0
    for axis_at, blocks in cuts:
        steps = jax.random.uniform(jax.random.fold_in(jax.random.fold_in(stream_key, 6), axis_at), (blocks,), jnp.float32, least / len(cuts), top_value / len(cuts))
        level = level * jnp.repeat(jnp.exp(steps), extent[axis_at] // blocks).reshape((-1,) + (1,) * (len(extent) - 1 - axis_at))
    return level


def split_up(count, total, reach, skew):
    loads = [(1 << 20) // math.isqrt(grade ** skew) + 1 for grade in range(2, count + 1)]
    spare, counts = total - reach - (count - 1), [1] * (count - 1)
    while spare > 0:
        candidates = [i for i in range(count - 1) if counts[i] < reach]
        pool, left = sum([loads[i] for i in candidates]), spare
        for i in candidates:
            extra = min(reach - counts[i], max(1, left * loads[i] // pool), spare)
            counts[i] = counts[i] + extra
            spare = spare - extra
    return np.array([reach] + counts)


def uneven(rng, count, total, bound, lean):
    if count == 2:
        one = jax.random.randint(rng, (), max(1, total - bound), min(bound, total - 1) + 1)
        return jnp.stack([one, total - one])
    sizes = jnp.asarray(split_up(count, total, bound, lean), jnp.int32)
    twos = (count - 1) // 2
    source_of, receiver = sizes[1:1 + 2 * twos:2], sizes[2:2 + 2 * twos:2]
    margin = jnp.minimum(source_of - 1, bound - receiver)
    moved = jax.random.randint(jax.random.fold_in(rng, 1), (twos,), 0, 1 << 20) % (margin + 1)
    sizes = sizes.at[1:1 + 2 * twos:2].set(source_of - moved).at[2:2 + 2 * twos:2].set(receiver + moved)
    return sizes[jax.random.permutation(jax.random.fold_in(rng, 2), count)]


def centred(key, extent, width, bound, cuts=(), dtype=jnp.bfloat16):
    result = width * jax.random.normal(key, extent, jnp.float32)
    if cuts:
        result = result * shard_levels(key, extent, cuts, -0.22, 0.18)
    return jnp.clip(result, -bound, bound).astype(dtype)


def setup_inputs(seed: int = 0) -> dict:
    arg_keys = jax.random.split(jax.random.key(seed), 4)
    momentum = centred(arg_keys[0], (EXPERTS, DEVICES * CAP, R), 1.0, 6.0, ((1, 128),))
    lengths = jax.vmap(lambda own: uneven(own, DEVICES, C, CAP, 1))(jax.random.split(arg_keys[1], EXPERTS)).reshape((EXPERTS, DEVICES)).astype(jnp.int32)
    weight = centred(arg_keys[2], (EXPERTS, DEVICES * CAP, R), 1.0, 6.0, ((1, 128),), jnp.float32)
    return {"momentum": momentum, "lengths": lengths, "weight": weight}


quintic_first = 3.4445
quintic_second = -4.775
quintic_third = 2.0315
margin_square = 2.25
epsilon_norm = 1e-06
learn_rate = 0.02
decay_rate = 0.1

def one_expert(live_rows):
    gram_total = jnp.dot(live_rows.T, live_rows, preferred_element_type=jnp.float32)
    norm_scale = margin_square / (jnp.sqrt(jnp.sum(gram_total * gram_total)) + epsilon_norm)
    gram_round = gram_total.astype(jnp.bfloat16)
    scaled = (live_rows.astype(jnp.float32) * jnp.sqrt(norm_scale)).astype(jnp.bfloat16)
    first_term = jnp.dot(scaled, gram_round, preferred_element_type=jnp.float32)
    second_term = jnp.dot(first_term.astype(jnp.bfloat16), gram_round, preferred_element_type=jnp.float32)
    combined = quintic_first * scaled.astype(jnp.float32) + quintic_second * norm_scale * first_term + quintic_third * norm_scale * norm_scale * second_term
    return (math.sqrt(C) * combined).astype(jnp.bfloat16)

def reference(momentum, lengths, weight):
    slot_index = lax.broadcasted_iota(jnp.int32, (EXPERTS, DEVICES * CAP), 1) % CAP
    limits = jnp.repeat(lengths, CAP, axis=1)
    live_rows = jnp.where((slot_index < limits)[:, :, None], momentum, jnp.zeros((), jnp.bfloat16))
    update = lax.map(one_expert, live_rows)
    new_weight = weight * (1.0 - learn_rate * decay_rate) - learn_rate * update.astype(jnp.float32)
    return (update, new_weight)
```

```python
import functools
import math

import jax
import jax.numpy as jnp
from jax import lax
from jax.experimental import pallas as pl
from jax.experimental.pallas import tpu as pltpu
from jax.sharding import PartitionSpec as P

C = 7168
R = 2048
CAP = 112
AXES = ("group", "col")

quintic_first = 3.4445
quintic_second = -4.775
quintic_third = 2.0315
margin_square = 2.25
epsilon_norm = 1e-06
learn_rate = 0.02
decay_rate = 0.1

BLOCK = 256
SLOTS = 18
HALF = SLOTS * BLOCK
ROUTE = HALF // 2
CHUNK = ROUTE // 4
PIECE = CHUNK // 4
SAME = [(a, b) for a in range(4) for b in range(a, 4)]


def pairs(move):
    def place(x, y, z, c):
        return (x % 4) * 32 + (y % 4) * 8 + (z % 4) * 2 + c

    return [
        (place(x, y, z, c), place(*move(x, y, z, c)))
        for x in range(4) for y in range(4) for z in range(4) for c in range(2)
    ]


def flipped(steps):
    return [(b, a) for a, b in steps]


def to_expert(d):
    def move(x, y, z, c):
        if d == 2:
            return (x + 1, y + 1, z, c) if c == 0 else (x - 1, y - 1, z, c)
        d1 = 1 if d == 1 else -1
        return (x + d1, y, z, c) if c == 0 else (x, y + d1, z, c)

    return pairs(move)


RING_P = {k: pairs(lambda x, y, z, c, k=k: (x + k, y - k, z, c)) for k in (1, 2, 3)}
RING_Q = {k: pairs(lambda x, y, z, c, k=k: (x, y, z + k, c)) for k in (1, 2, 3)}
OTHER_CORE = pairs(lambda x, y, z, c: (x, y, z, 1 - c))


def shift(value, steps):
    return lax.ppermute(value, AXES, steps)


def gram_kernel(place, *refs):
    rows, outs = refs[:8], refs[8:16]
    x_all, x_turned, blocks, in_sems, out_sems = refs[16:]
    core, p, q = place[0], place[1], place[2]
    loads = [
        pltpu.make_async_copy(rows[i], x_all.at[pl.ds(CAP * i, CAP)], in_sems.at[i])
        for i in range(8)
    ]
    for load in loads:
        load.start()
    for load in loads:
        load.wait()

    def columns(at):
        return pl.ds(pl.multiple_of(at * BLOCK, BLOCK), BLOCK)

    for a in range(4):
        x_turned[a * BLOCK:(a + 1) * BLOCK, :] = x_all[:, columns(core * 4 + a)].T
    for slot in range(SLOTS):
        if slot < 10:
            a, b = SAME[slot]
            left = x_turned[a * BLOCK:(a + 1) * BLOCK, :]
            at = core * 4 + b
        else:
            s = slot - 10
            a = jnp.where(core == 0, s // 2, 2 + s // 4)
            left = x_turned[columns(a), :]
            at = jnp.where(core == 0, 4 + s % 2, s % 4)
        blocks[slot * BLOCK:(slot + 1) * BLOCK, :] = jnp.dot(
            left, x_all[:, columns(at)], preferred_element_type=jnp.float32
        ).astype(jnp.bfloat16)
    stores = []
    for route, own in ((0, p), (1, q)):
        for k in range(4):
            start = route * ROUTE + lax.rem(own + k, 4) * CHUNK
            stores.append(pltpu.make_async_copy(
                blocks.at[pl.ds(pl.multiple_of(start, 16), CHUNK)],
                outs[route * 4 + k],
                out_sems.at[route * 4 + k],
            ))
    for store in stores:
        store.start()
    for store in stores:
        store.wait()


def gram(place, rows):
    anywhere = pl.BlockSpec(memory_space=pl.ANY)
    return pl.pallas_call(
        gram_kernel,
        out_shape=[jax.ShapeDtypeStruct((CHUNK, BLOCK), jnp.bfloat16)] * 8,
        in_specs=[pl.BlockSpec(memory_space=pltpu.SMEM)] + [anywhere] * 8,
        out_specs=[anywhere] * 8,
        scratch_shapes=[
            pltpu.VMEM((8 * CAP, R), jnp.bfloat16),
            pltpu.VMEM((4 * BLOCK, 8 * CAP), jnp.bfloat16),
            pltpu.VMEM((HALF, BLOCK), jnp.bfloat16),
            pltpu.SemaphoreType.DMA((8,)),
            pltpu.SemaphoreType.DMA((8,)),
        ],
        compiler_params=pltpu.CompilerParams(vmem_limit_bytes=40 << 20),
        name="gram",
    )(place, *rows)


def stored_at(i, j):
    if i // 4 == j // 4:
        a, b = i % 4, j % 4
        return i // 4, SAME.index((min(a, b), max(a, b))), a > b
    low, high = min(i, j), max(i, j)
    if high < 6:
        return 0, 10 + 2 * low + (high - 4), i > j
    return 1, 10 + 4 * (high - 6) + low, i < j


def update_kernel(place, *refs):
    rows, chunks, outs = refs[:4], refs[4:20], refs[20:24]
    x_all, blocks, first, first_round, in_sems = refs[24:]
    core, p, q = place[0], place[1], place[2]
    loads = [
        pltpu.make_async_copy(rows[i], x_all.at[pl.ds(CAP * i, CAP)], in_sems.at[i])
        for i in range(4)
    ]
    for side in range(2):
        half = core if side == 0 else 1 - core
        for route, own in ((0, p), (1, q)):
            for k in range(4):
                i = side * 8 + route * 4 + k
                start = half * HALF + route * ROUTE + lax.rem(own + 4 - k, 4) * CHUNK
                loads.append(pltpu.make_async_copy(
                    chunks[i],
                    blocks.at[pl.ds(pl.multiple_of(start, 16), CHUNK)],
                    in_sems.at[4 + i],
                ))
    for load in loads:
        load.start()
    for load in loads:
        load.wait()

    def block(half, slot):
        start = half * HALF + slot * BLOCK
        return blocks[start:start + BLOCK, :]

    def times_gram(left, j):
        total = None
        for i in range(8):
            half, slot, turned = stored_at(i, j)
            term = lax.dot_general(
                left[:, i * BLOCK:(i + 1) * BLOCK],
                block(half, slot),
                (((1,), (1 if turned else 0,)), ((), ())),
                preferred_element_type=jnp.float32,
            )
            total = term if total is None else total + term
        return total

    squares = jnp.zeros((BLOCK, BLOCK), jnp.float32)
    for half in range(2):
        for slot in range(SLOTS):
            value = block(half, slot).astype(jnp.float32)
            diagonal = slot < 10 and SAME[slot][0] == SAME[slot][1]
            squares += value * value * (1.0 if diagonal else 2.0)
    total = jnp.sum(squares, axis=(0, 1), keepdims=True)
    norm_scale = margin_square / (jnp.sqrt(total) + epsilon_norm)
    root = jnp.sqrt(norm_scale)

    for j in range(8):
        at = slice(j * BLOCK, (j + 1) * BLOCK)
        value = times_gram(x_all, j)
        first[:, at] = value
        first_round[:, at] = value.astype(jnp.bfloat16)
    for j in range(8):
        at = slice(j * BLOCK, (j + 1) * BLOCK)
        second = times_gram(first_round, j)
        scaled = (x_all[:, at].astype(jnp.float32) * root).astype(jnp.bfloat16)
        combined = (
            quintic_first * scaled.astype(jnp.float32)
            + (quintic_second * norm_scale * root) * first[:, at]
            + (quintic_third * norm_scale * norm_scale * root) * second
        )
        value = (math.sqrt(C) * combined).astype(jnp.bfloat16)
        for d in range(4):
            outs[d][:, at] = value[CAP * d:CAP * (d + 1)]


def update(place, rows, chunks):
    anywhere = pl.BlockSpec(memory_space=pl.ANY)
    return pl.pallas_call(
        update_kernel,
        out_shape=[jax.ShapeDtypeStruct((CAP, R), jnp.bfloat16)] * 4,
        in_specs=[pl.BlockSpec(memory_space=pltpu.SMEM)] + [anywhere] * 20,
        out_specs=[pl.BlockSpec(memory_space=pltpu.VMEM)] * 4,
        scratch_shapes=[
            pltpu.VMEM((4 * CAP, R), jnp.bfloat16),
            pltpu.VMEM((2 * HALF, BLOCK), jnp.bfloat16),
            pltpu.VMEM((4 * CAP, R), jnp.float32),
            pltpu.VMEM((4 * CAP, R), jnp.bfloat16),
            pltpu.SemaphoreType.DMA((20,)),
        ],
        compiler_params=pltpu.CompilerParams(vmem_limit_bytes=48 << 20),
        name="update",
    )(place, *rows, *chunks)


def apply_kernel(home, a0, a1, a2, a3, weight, out, new_weight):
    step = pl.program_id(0)
    for d, ref in enumerate((a0, a1, a2, a3)):
        @pl.when(step == d)
        def _(ref=ref):
            value = ref[...]
            out[0] = value
            new_weight[0] = (
                weight[0] * (1.0 - learn_rate * decay_rate)
                - learn_rate * value.astype(jnp.float32)
            )


def apply(home, returned, weight):
    whole = pl.BlockSpec((CAP, R), lambda d, h: (0, 0))
    one = pl.BlockSpec((1, CAP, R), lambda d, h: (lax.rem(h[0] + d, 4), 0, 0))
    return pl.pallas_call(
        apply_kernel,
        out_shape=[
            jax.ShapeDtypeStruct((4, CAP, R), jnp.bfloat16),
            jax.ShapeDtypeStruct((4, CAP, R), jnp.float32),
        ],
        grid_spec=pltpu.PrefetchScalarGridSpec(
            num_scalar_prefetch=1,
            grid=(4,),
            in_specs=[whole] * 4 + [one],
            out_specs=[one, one],
        ),
        compiler_params=pltpu.CompilerParams(vmem_limit_bytes=32 << 20),
        name="apply",
    )(home, *returned, weight)


def summed(parts, at=None):
    total = None
    for part in parts:
        if at is not None:
            part = lax.dynamic_index_in_dim(part, at, 0, keepdims=False)
        part = part.astype(jnp.float32)
        total = part if total is None else total + part
    return total.astype(jnp.bfloat16)


def on_device(momentum, lengths, weight):
    x, col = lax.axis_index("group"), lax.axis_index("col")
    y, z, core = col // 8, col // 2 % 4, col % 2
    home = (x + y) % 4
    place = jnp.stack([core, x, z]).astype(jnp.int32)
    slot_index = lax.broadcasted_iota(jnp.int32, (CAP, R), 0)

    def live(d):
        e = (home + d) % 4
        rows = lax.dynamic_index_in_dim(momentum, e, 0, keepdims=False)
        limit = lax.dynamic_index_in_dim(lengths, e, 0, keepdims=False)
        return jnp.where(slot_index < limit, rows, jnp.zeros((), jnp.bfloat16))

    routes = {d: to_expert(d) for d in (1, 2, 3)}
    rows = [live(0)] + [shift(live(d), routes[d]) for d in (1, 2, 3)]
    other_rows = [shift(part, OTHER_CORE) for part in rows]

    parts = gram(place, rows + other_rows)
    parts = [part.reshape(4, PIECE, BLOCK) for part in parts]
    ring_of = ((RING_P, RING_Q), (RING_Q, RING_P))
    own_of = ((x, z), (z, x))
    summed_one = []
    for route in range(2):
        mine = parts[route * 4:route * 4 + 4]
        summed_one.append([mine[0]] + [shift(mine[k], ring_of[route][0][k]) for k in (1, 2, 3)])
    pieces = []
    for route in range(2):
        own = own_of[route][1]
        send = [summed(summed_one[route], (own + k) % 4) for k in range(4)]
        arrived = [send[0]] + [shift(send[k], ring_of[route][1][k]) for k in (1, 2, 3)]
        pieces.append(arrived)
    pieces = [summed(arrived) for arrived in pieces]

    chunks = []
    for route in range(2):
        own = own_of[route][1]
        chunk = jnp.zeros((4, PIECE, BLOCK), jnp.bfloat16)
        got = [pieces[route]] + [shift(pieces[route], ring_of[route][1][k]) for k in (1, 2, 3)]
        for k in range(4):
            chunk = lax.dynamic_update_index_in_dim(chunk, got[k], (own + 4 - k) % 4, 0)
        chunks.append(chunk.reshape(CHUNK, BLOCK))
    mine = []
    for route in range(2):
        mine += [chunks[route]]
        mine += [shift(chunks[route], ring_of[route][0][k]) for k in (1, 2, 3)]
    others = [shift(chunk, OTHER_CORE) for chunk in mine]

    updates = update(place, rows, mine + others)
    returned = [updates[0]] + [shift(updates[d], flipped(routes[d])) for d in (1, 2, 3)]
    return tuple(apply(home.reshape(1).astype(jnp.int32), returned, weight))


def solution(mesh):
    placed = (
        P(None, ("group", "col"), None),
        P(None, ("group", "col")),
        P(None, ("group", "col"), None),
    )
    return jax.shard_map(
        on_device,
        mesh=mesh,
        in_specs=placed,
        out_specs=(P(None, ("group", "col"), None), P(None, ("group", "col"), None)),
        check_vma=False,
    )
```

```python
import functools
import math

import jax
import jax.numpy as jnp
from jax import lax
from jax.experimental import pallas as pl
from jax.experimental.pallas import tpu as pltpu
from jax.sharding import PartitionSpec as P

C = 7168
R = 2048
CAP = 112
AXES = ("group", "col")

quintic_first = 3.4445
quintic_second = -4.775
quintic_third = 2.0315
margin_square = 2.25
epsilon_norm = 1e-06
learn_rate = 0.02
decay_rate = 0.1

BLOCK = 256
SLOTS = 18
HALF = SLOTS * BLOCK
ROUTE = HALF // 2
CHUNK = ROUTE // 4
SAME = [(a, b) for a in range(4) for b in range(a, 4)]


def pairs(move):
    def place(x, y, z, c):
        return (x % 4) * 32 + (y % 4) * 8 + (z % 4) * 2 + c

    return [
        (place(x, y, z, c), place(*move(x, y, z, c)))
        for x in range(4) for y in range(4) for z in range(4) for c in range(2)
    ]


def flipped(steps):
    return [(b, a) for a, b in steps]


def to_expert(d):
    def move(x, y, z, c):
        along_x = (c == 0) != (d == 2)
        return (x + d, y, z, c) if along_x else (x, y + d, z, c)

    return pairs(move)


RING_P = {k: pairs(lambda x, y, z, c, k=k: (x + k, y - k, z, c)) for k in (1, 2, 3)}
RING_Q = {k: pairs(lambda x, y, z, c, k=k: (x, y, z + k, c)) for k in (1, 2, 3)}
OTHER_CORE = pairs(lambda x, y, z, c: (x, y, z, 1 - c))


def shift(value, steps):
    return lax.ppermute(value, AXES, steps)


def live_kernel(place, lengths, momentum, o0, o1, o2, o3, rows, sems):
    home = place[3]
    outs = (o0, o1, o2, o3)
    experts = [lax.rem(home + d, 4) for d in range(4)]
    loads = [
        pltpu.make_async_copy(momentum.at[experts[d]], rows.at[d], sems.at[d])
        for d in range(4)
    ]
    for load in loads:
        load.start()
    for d in (2, 1, 3, 0):
        loads[d].wait()
        slot = lax.broadcasted_iota(jnp.int32, (CAP, 128), 0)
        keep = slot < lengths[experts[d]]
        for at in range(0, R, 128):
            value = rows[d, :, at:at + 128]
            outs[d][:, at:at + 128] = jnp.where(keep, value, jnp.zeros_like(value))


def live(place, lengths, momentum):
    return pl.pallas_call(
        live_kernel,
        out_shape=[jax.ShapeDtypeStruct((CAP, R), jnp.bfloat16)] * 4,
        in_specs=[
            pl.BlockSpec(memory_space=pltpu.SMEM),
            pl.BlockSpec(memory_space=pltpu.SMEM),
            pl.BlockSpec(memory_space=pl.ANY),
        ],
        out_specs=[pl.BlockSpec(memory_space=pltpu.VMEM)] * 4,
        scratch_shapes=[
            pltpu.VMEM((4, CAP, R), jnp.bfloat16),
            pltpu.SemaphoreType.DMA((4,)),
        ],
        compiler_params=pltpu.CompilerParams(vmem_limit_bytes=16 << 20),
        name="live",
    )(place, lengths, momentum)


def gram_kernel(place, *refs):
    rows, outs = refs[:8], refs[8:16]
    x_all, x_turned, blocks, in_sems, out_sems = refs[16:]
    core, p, q = place[0], place[1], place[2]
    loads = [
        pltpu.make_async_copy(rows[i], x_all.at[pl.ds(CAP * i, CAP)], in_sems.at[i])
        for i in range(8)
    ]
    for load in loads:
        load.start()
    for load in loads:
        load.wait()

    def columns(at):
        return pl.ds(pl.multiple_of(at * BLOCK, BLOCK), BLOCK)

    for a in range(4):
        x_turned[a * BLOCK:(a + 1) * BLOCK, :] = x_all[:, columns(core * 4 + a)].T
    for slot in range(SLOTS):
        if slot < 10:
            a, b = SAME[slot]
            left = x_turned[a * BLOCK:(a + 1) * BLOCK, :]
            at = core * 4 + b
        else:
            s = slot - 10
            a = jnp.where(core == 0, s // 2, 2 + s // 4)
            left = x_turned[columns(a), :]
            at = jnp.where(core == 0, 4 + s % 2, s % 4)
        blocks[slot * BLOCK:(slot + 1) * BLOCK, :] = jnp.dot(
            left, x_all[:, columns(at)], preferred_element_type=jnp.float32
        ).astype(jnp.bfloat16)
    stores = []
    for route, own in ((0, p), (1, q)):
        for k in range(4):
            start = route * ROUTE + lax.rem(own + k, 4) * CHUNK
            stores.append(pltpu.make_async_copy(
                blocks.at[pl.ds(pl.multiple_of(start, 16), CHUNK)],
                outs[route * 4 + k],
                out_sems.at[route * 4 + k],
            ))
    for store in stores:
        store.start()
    for store in stores:
        store.wait()


def gram(place, rows):
    anywhere = pl.BlockSpec(memory_space=pl.ANY)
    return pl.pallas_call(
        gram_kernel,
        out_shape=[jax.ShapeDtypeStruct((CHUNK, BLOCK), jnp.bfloat16)] * 8,
        in_specs=[pl.BlockSpec(memory_space=pltpu.SMEM)] + [anywhere] * 8,
        out_specs=[anywhere] * 8,
        scratch_shapes=[
            pltpu.VMEM((8 * CAP, R), jnp.bfloat16),
            pltpu.VMEM((4 * BLOCK, 8 * CAP), jnp.bfloat16),
            pltpu.VMEM((HALF, BLOCK), jnp.bfloat16),
            pltpu.SemaphoreType.DMA((8,)),
            pltpu.SemaphoreType.DMA((8,)),
        ],
        compiler_params=pltpu.CompilerParams(vmem_limit_bytes=40 << 20),
        name="gram",
    )(place, *rows)


def stored_at(i, j):
    if i // 4 == j // 4:
        a, b = i % 4, j % 4
        return i // 4, SAME.index((min(a, b), max(a, b))), a > b
    low, high = min(i, j), max(i, j)
    if high < 6:
        return 0, 10 + 2 * low + (high - 4), i > j
    return 1, 10 + 4 * (high - 6) + low, i < j


def update_kernel(place, *refs):
    rows, chunks, outs = refs[:4], refs[4:20], refs[20:24]
    x_all, blocks, first, first_round, in_sems = refs[24:]
    core, p, q = place[0], place[1], place[2]
    loads = [
        pltpu.make_async_copy(rows[i], x_all.at[pl.ds(CAP * i, CAP)], in_sems.at[i])
        for i in range(4)
    ]
    for side in range(2):
        half = core if side == 0 else 1 - core
        for route, own in ((0, p), (1, q)):
            for k in range(4):
                i = side * 8 + route * 4 + k
                start = half * HALF + route * ROUTE + lax.rem(own + 4 - k, 4) * CHUNK
                loads.append(pltpu.make_async_copy(
                    chunks[i],
                    blocks.at[pl.ds(pl.multiple_of(start, 16), CHUNK)],
                    in_sems.at[4 + i],
                ))
    for load in loads:
        load.start()
    for load in loads:
        load.wait()

    def block(half, slot):
        start = half * HALF + slot * BLOCK
        return blocks[start:start + BLOCK, :]

    def times_gram(left, j):
        total = None
        for i in range(8):
            half, slot, turned = stored_at(i, j)
            term = lax.dot_general(
                left[:, i * BLOCK:(i + 1) * BLOCK],
                block(half, slot),
                (((1,), (1 if turned else 0,)), ((), ())),
                preferred_element_type=jnp.float32,
            )
            total = term if total is None else total + term
        return total

    squares = jnp.zeros((BLOCK, BLOCK), jnp.float32)
    for half in range(2):
        for slot in range(SLOTS):
            value = block(half, slot).astype(jnp.float32)
            diagonal = slot < 10 and SAME[slot][0] == SAME[slot][1]
            squares += value * value * (1.0 if diagonal else 2.0)
    total = jnp.sum(squares, axis=(0, 1), keepdims=True)
    norm_scale = margin_square / (jnp.sqrt(total) + epsilon_norm)
    root = jnp.sqrt(norm_scale)

    for j in range(8):
        at = slice(j * BLOCK, (j + 1) * BLOCK)
        value = times_gram(x_all, j)
        first[:, at] = value
        first_round[:, at] = value.astype(jnp.bfloat16)
    for j in range(8):
        at = slice(j * BLOCK, (j + 1) * BLOCK)
        second = times_gram(first_round, j)
        scaled = (x_all[:, at].astype(jnp.float32) * root).astype(jnp.bfloat16)
        combined = (
            quintic_first * scaled.astype(jnp.float32)
            + (quintic_second * norm_scale * root) * first[:, at]
            + (quintic_third * norm_scale * norm_scale * root) * second
        )
        value = (math.sqrt(C) * combined).astype(jnp.bfloat16)
        for d in range(4):
            outs[d][:, at] = value[CAP * d:CAP * (d + 1)]


def update(place, rows, chunks):
    anywhere = pl.BlockSpec(memory_space=pl.ANY)
    return pl.pallas_call(
        update_kernel,
        out_shape=[jax.ShapeDtypeStruct((CAP, R), jnp.bfloat16)] * 4,
        in_specs=[pl.BlockSpec(memory_space=pltpu.SMEM)] + [anywhere] * 20,
        out_specs=[pl.BlockSpec(memory_space=pltpu.VMEM)] * 4,
        scratch_shapes=[
            pltpu.VMEM((4 * CAP, R), jnp.bfloat16),
            pltpu.VMEM((2 * HALF, BLOCK), jnp.bfloat16),
            pltpu.VMEM((4 * CAP, R), jnp.float32),
            pltpu.VMEM((4 * CAP, R), jnp.bfloat16),
            pltpu.SemaphoreType.DMA((20,)),
        ],
        compiler_params=pltpu.CompilerParams(vmem_limit_bytes=48 << 20),
        name="update",
    )(place, *rows, *chunks)


def apply_kernel(home, a0, a1, a2, a3, weight, out, new_weight):
    step = pl.program_id(0)
    for d, ref in enumerate((a0, a1, a2, a3)):
        @pl.when(step == d)
        def _(ref=ref):
            value = ref[...]
            out[0] = value
            new_weight[0] = (
                weight[0] * (1.0 - learn_rate * decay_rate)
                - learn_rate * value.astype(jnp.float32)
            )


def apply(home, returned, weight):
    whole = pl.BlockSpec((CAP, R), lambda d, h: (0, 0))
    one = pl.BlockSpec((1, CAP, R), lambda d, h: (lax.rem(h[0] + d, 4), 0, 0))
    return pl.pallas_call(
        apply_kernel,
        out_shape=[
            jax.ShapeDtypeStruct((4, CAP, R), jnp.bfloat16),
            jax.ShapeDtypeStruct((4, CAP, R), jnp.float32),
        ],
        grid_spec=pltpu.PrefetchScalarGridSpec(
            num_scalar_prefetch=1,
            grid=(4,),
            in_specs=[whole] * 4 + [one],
            out_specs=[one, one],
        ),
        compiler_params=pltpu.CompilerParams(vmem_limit_bytes=32 << 20),
        name="apply",
    )(home, *returned, weight)


def summed(parts):
    total = None
    for part in parts:
        part = part.astype(jnp.float32)
        total = part if total is None else total + part
    return total.astype(jnp.bfloat16)


def on_device(momentum, lengths, weight):
    x, col = lax.axis_index("group"), lax.axis_index("col")
    y, z, core = col // 8, col // 2 % 4, col % 2
    home = (x + y) % 4
    place = jnp.stack([core, x, z, home]).astype(jnp.int32)

    routes = {d: to_expert(d) for d in (1, 2, 3)}
    rows = live(place, lengths.reshape(4), momentum)
    rows = [rows[0]] + [shift(rows[d], routes[d]) for d in (1, 2, 3)]
    other_rows = [shift(part, OTHER_CORE) for part in rows]

    parts = gram(place, rows + other_rows)
    rings = (RING_P, RING_Q)
    chunks = []
    for route in range(2):
        mine = parts[route * 4:route * 4 + 4]
        chunks.append([mine[0]] + [shift(mine[k], rings[route][k]) for k in (1, 3, 2)])
    chunks = [summed(got) for got in chunks]
    chunks = [
        [chunks[route]] + [shift(chunks[route], rings[1 - route][k]) for k in (1, 3, 2)]
        for route in range(2)
    ]
    chunks = [summed(got) for got in chunks]
    mine = []
    for route in range(2):
        mine += [chunks[route]] + [shift(chunks[route], rings[route][k]) for k in (1, 2, 3)]
    others = [shift(chunk, OTHER_CORE) for chunk in mine]

    updates = update(place, rows, mine + others)
    returned = [updates[0]] + [shift(updates[d], flipped(routes[d])) for d in (1, 2, 3)]
    return tuple(apply(home.reshape(1).astype(jnp.int32), returned, weight))


def solution(mesh):
    placed = (
        P(None, ("group", "col"), None),
        P(None, ("group", "col")),
        P(None, ("group", "col"), None),
    )
    return jax.shard_map(
        on_device,
        mesh=mesh,
        in_specs=placed,
        out_specs=(P(None, ("group", "col"), None), P(None, ("group", "col"), None)),
        check_vma=False,
    )
```

```python
import functools
import math

import jax
import jax.numpy as jnp
from jax import lax
from jax.experimental import pallas as pl
from jax.experimental.pallas import tpu as pltpu
from jax.sharding import PartitionSpec as P

C = 7168
R = 2048
CAP = 112
AXES = ("group", "col")

quintic_first = 3.4445
quintic_second = -4.775
quintic_third = 2.0315
margin_square = 2.25
epsilon_norm = 1e-06
learn_rate = 0.02
decay_rate = 0.1

BLOCK = 256
HALF_BLOCK = BLOCK // 2
SAME = [(a, b) for a in range(4) for b in range(a + 1, 4)]
OFF = 14
SLOTS = OFF + 4
TOPS = OFF * BLOCK
CORNERS = TOPS + 4 * HALF_BLOCK
HALF = CORNERS + 2 * HALF_BLOCK
ROUTE = HALF // 2
CHUNK = ROUTE // 4


def pairs(move):
    def place(x, y, z, c):
        return (x % 4) * 32 + (y % 4) * 8 + (z % 4) * 2 + c

    return [
        (place(x, y, z, c), place(*move(x, y, z, c)))
        for x in range(4) for y in range(4) for z in range(4) for c in range(2)
    ]


def flipped(steps):
    return [(b, a) for a, b in steps]


def to_expert(d):
    def move(x, y, z, c):
        along_x = (c == 0) != (d == 2)
        return (x + d, y, z, c) if along_x else (x, y + d, z, c)

    return pairs(move)


RING_P = {k: pairs(lambda x, y, z, c, k=k: (x + k, y - k, z, c)) for k in (1, 2, 3)}
RING_Q = {k: pairs(lambda x, y, z, c, k=k: (x, y, z + k, c)) for k in (1, 2, 3)}
OTHER_CORE = pairs(lambda x, y, z, c: (x, y, z, 1 - c))


def shift(value, steps):
    return lax.ppermute(value, AXES, steps)


def places():
    x, col = lax.axis_index("group"), lax.axis_index("col")
    return col % 2, x, col // 2 % 4, (x + col // 8) % 4


def live_kernel(lengths, momentum, o0, o1, o2, o3, rows, sems):
    home = places()[3]
    outs = (o0, o1, o2, o3)
    experts = [lax.rem(home + d, 4) for d in range(4)]
    loads = [
        pltpu.make_async_copy(momentum.at[experts[d]], rows.at[d], sems.at[d])
        for d in range(4)
    ]
    for load in loads:
        load.start()
    lane = lax.broadcasted_iota(jnp.int32, (1, 4), 1)
    for d in (1, 2, 3, 0):
        loads[d].wait()
        slot = lax.broadcasted_iota(jnp.int32, (CAP, 128), 0)
        keep = slot < jnp.sum(jnp.where(lane == experts[d], lengths[...], 0))
        for at in range(0, R, 128):
            value = rows[d, :, at:at + 128]
            outs[d][:, at:at + 128] = jnp.where(keep, value, jnp.zeros_like(value))


def live(lengths, momentum):
    return pl.pallas_call(
        live_kernel,
        out_shape=[jax.ShapeDtypeStruct((CAP, R), jnp.bfloat16)] * 4,
        in_specs=[
            pl.BlockSpec(memory_space=pltpu.VMEM),
            pl.BlockSpec(memory_space=pltpu.HBM),
        ],
        out_specs=[pl.BlockSpec(memory_space=pltpu.VMEM)] * 4,
        scratch_shapes=[
            pltpu.VMEM((4, CAP, R), jnp.bfloat16),
            pltpu.SemaphoreType.DMA((4,)),
        ],
        compiler_params=pltpu.CompilerParams(vmem_limit_bytes=61 << 20),
        name="live",
    )(lengths, momentum)


def gram_kernel(count, first_stage, last_stage, *refs):
    rows, rest = refs[:count], refs[count:]
    if not first_stage:
        before, rest = rest[0], rest[1:]
    if last_stage:
        outs, rest = rest[:8], rest[8:]
        blocks, out_sems = rest[-2:]
    else:
        total, rest = rest[0], rest[1:]
    x_all, x_turned, in_sems = rest[:3]
    core, p, q, _ = places()
    loads = [
        pltpu.make_async_copy(rows[i], x_all.at[pl.ds(CAP * i, CAP)], in_sems.at[i])
        for i in range(count)
    ]
    for load in loads:
        load.start()
    for load in loads:
        load.wait()

    def columns(at):
        return pl.ds(pl.multiple_of(at * BLOCK, BLOCK), BLOCK)

    for a in range(4):
        x_turned[a * BLOCK:(a + 1) * BLOCK, :] = x_all[:, columns(core * 4 + a)].T
    for slot in range(SLOTS):
        a, b = SAME[slot] if slot < 6 else (slot - OFF, slot - OFF)
        at = core * 4 + b
        if 6 <= slot < OFF:
            s = slot - 6
            a = jnp.where(core == 0, s // 2, 2 + s // 4)
            at = jnp.where(core == 0, 4 + s % 2, s % 4)
        value = jnp.dot(
            x_turned[columns(a), :], x_all[:, columns(at)], preferred_element_type=jnp.float32
        )
        here = slice(slot * BLOCK, (slot + 1) * BLOCK)
        if not first_stage:
            value = value + before[here, :]
        if not last_stage:
            total[here, :] = value
            continue
        value = value.astype(jnp.bfloat16)
        if slot < OFF:
            blocks[here, :] = value
        else:
            top = TOPS + a * HALF_BLOCK
            blocks[top:top + HALF_BLOCK, :] = value[:HALF_BLOCK]
            corner, side = CORNERS + a // 2 * HALF_BLOCK, a % 2 * HALF_BLOCK
            blocks[corner:corner + HALF_BLOCK, side:side + HALF_BLOCK] = value[HALF_BLOCK:, HALF_BLOCK:]
    if not last_stage:
        return
    stores = []
    for route, own in ((0, p), (1, q)):
        for k in range(4):
            start = route * ROUTE + lax.rem(own + k, 4) * CHUNK
            stores.append(pltpu.make_async_copy(
                blocks.at[pl.ds(pl.multiple_of(start, 16), CHUNK)],
                outs[route * 4 + k],
                out_sems.at[route * 4 + k],
            ))
    for store in stores:
        store.start()
    for store in stores:
        store.wait()


def gram(rows, before=None, last=False, weight=1):
    count, depth = len(rows), len(rows) * CAP
    vmem = pl.BlockSpec(memory_space=pltpu.VMEM)
    anywhere = pl.BlockSpec(memory_space=pl.ANY)
    scratch = [
        pltpu.VMEM((depth, R), jnp.bfloat16),
        pltpu.VMEM((4 * BLOCK, depth), jnp.bfloat16),
        pltpu.SemaphoreType.DMA((count,)),
    ]
    if last:
        out_shape = [jax.ShapeDtypeStruct((CHUNK, BLOCK), jnp.bfloat16)] * 8
        scratch += [pltpu.VMEM((HALF, BLOCK), jnp.bfloat16), pltpu.SemaphoreType.DMA((8,))]
    else:
        out_shape = jax.ShapeDtypeStruct((SLOTS * BLOCK, BLOCK), jnp.float32)
    operands = list(rows) + ([] if before is None else [before])
    return pl.pallas_call(
        functools.partial(gram_kernel, count, before is None, last),
        out_shape=out_shape,
        in_specs=[anywhere] * count + [vmem] * (before is not None),
        out_specs=[anywhere] * 8 if last else vmem,
        scratch_shapes=scratch,
        input_output_aliases={count: 0} if before is not None and not last else {},
        compiler_params=pltpu.CompilerParams(vmem_limit_bytes=16 << 20),
        cost_estimate=pl.CostEstimate(
            flops=2 * SLOTS * BLOCK * BLOCK * depth * weight,
            bytes_accessed=depth * R * 2 + 2 * SLOTS * BLOCK * BLOCK * 4,
            transcendentals=0,
        ),
        name="gram",
    )(*operands)


def stored_at(i, j):
    if i // 4 == j // 4:
        a, b = i % 4, j % 4
        return i // 4, SAME.index((min(a, b), max(a, b))), a > b
    low, high = min(i, j), max(i, j)
    if high < 6:
        return 0, 6 + 2 * low + (high - 4), i > j
    return 1, 6 + 4 * (high - 6) + low, i < j


def update_kernel(*refs):
    rows, chunks, outs = refs[:4], refs[4:18], refs[18:22]
    x_all, blocks, diagonal, first, first_round, in_sems, chunk_sems = refs[22:]
    core, p, q, _ = places()
    loads = [
        pltpu.make_async_copy(rows[i], x_all.at[pl.ds(CAP * i, CAP)], in_sems.at[i])
        for i in range(4)
    ]
    for side in range(2):
        half = core if side == 0 else 1 - core
        for route, own in ((0, p), (1, q)):
            for k in range(4):
                if side == 0:
                    chunk = chunks[route * 4 + k]
                elif k in (0, 3):
                    chunk = chunks[8 + route * 3].at[pl.ds(k // 3 * CHUNK, CHUNK)]
                else:
                    chunk = chunks[8 + route * 3 + 3 - k]
                number = half * 8 + route * 4 + lax.rem(own + 4 - k, 4)
                loads.append(pltpu.make_async_copy(
                    chunk,
                    blocks.at[pl.ds(pl.multiple_of(number * CHUNK, 16), CHUNK)],
                    chunk_sems.at[number],
                ))
    for load in loads:
        load.start()

    def block(half, slot):
        start = half * HALF + slot * BLOCK
        return blocks[start:start + BLOCK, :]

    def times_gram(left, j):
        total = None
        for i in range(8):
            if i == j:
                part, turned = diagonal[j * BLOCK:(j + 1) * BLOCK, :], False
            else:
                half, slot, turned = stored_at(i, j)
                part = block(half, slot)
            term = lax.dot_general(
                left[:, i * BLOCK:(i + 1) * BLOCK],
                part,
                (((1,), (1 if turned else 0,)), ((), ())),
                preferred_element_type=jnp.float32,
            )
            total = term if total is None else total + term
        return total

    def squared(value):
        value = value.astype(jnp.float32)
        return value * value

    twice = jnp.zeros((16, BLOCK), jnp.float32)
    once = jnp.zeros((HALF_BLOCK, HALF_BLOCK), jnp.float32)
    for number in range(16):
        here = blocks.at[pl.ds(number * CHUNK, CHUNK)]
        pltpu.make_async_copy(here, here, chunk_sems.at[number]).wait()
        for at in range(number * CHUNK, (number + 1) * CHUNK, 16):
            if at % HALF < TOPS:
                twice += squared(blocks[at:at + 16, :])
    for i in range(8):
        half, a = i // 4, i % 4
        start = half * HALF + TOPS + a * HALF_BLOCK
        corner, side = half * HALF + CORNERS + a // 2 * HALF_BLOCK, a % 2 * HALF_BLOCK
        top = blocks[start:start + HALF_BLOCK, :]
        last = blocks[corner:corner + HALF_BLOCK, side:side + HALF_BLOCK]
        diagonal[i * BLOCK:i * BLOCK + HALF_BLOCK, :] = top
        diagonal[i * BLOCK + HALF_BLOCK:(i + 1) * BLOCK, :HALF_BLOCK] = top[:, HALF_BLOCK:].T
        diagonal[i * BLOCK + HALF_BLOCK:(i + 1) * BLOCK, HALF_BLOCK:] = last
        once += squared(top[:, :HALF_BLOCK]) + squared(last) + 2.0 * squared(top[:, HALF_BLOCK:])
    total = 2.0 * jnp.sum(twice, axis=(0, 1), keepdims=True) + jnp.sum(once, axis=(0, 1), keepdims=True)
    norm_scale = margin_square / (jnp.sqrt(total) + epsilon_norm)
    root = jnp.sqrt(norm_scale)
    for load in loads[:4]:
        load.wait()

    for j in range(8):
        at = slice(j * BLOCK, (j + 1) * BLOCK)
        value = times_gram(x_all, j)
        first[:, at] = value
        first_round[:, at] = value.astype(jnp.bfloat16)
    for j in range(8):
        at = slice(j * BLOCK, (j + 1) * BLOCK)
        second = times_gram(first_round, j)
        scaled = (x_all[:, at].astype(jnp.float32) * root).astype(jnp.bfloat16)
        combined = (
            quintic_first * scaled.astype(jnp.float32)
            + (quintic_second * norm_scale * root) * first[:, at]
            + (quintic_third * norm_scale * norm_scale * root) * second
        )
        value = (math.sqrt(C) * combined).astype(jnp.bfloat16)
        for d in range(4):
            outs[d][:, at] = value[CAP * d:CAP * (d + 1)]


def update(rows, chunks):
    anywhere = pl.BlockSpec(memory_space=pl.ANY)
    return pl.pallas_call(
        update_kernel,
        out_shape=[jax.ShapeDtypeStruct((CAP, R), jnp.bfloat16)] * 4,
        in_specs=[anywhere] * 18,
        out_specs=[pl.BlockSpec(memory_space=pltpu.VMEM)] * 4,
        scratch_shapes=[
            pltpu.VMEM((4 * CAP, R), jnp.bfloat16),
            pltpu.VMEM((2 * HALF, BLOCK), jnp.bfloat16),
            pltpu.VMEM((R, BLOCK), jnp.bfloat16),
            pltpu.VMEM((4 * CAP, R), jnp.float32),
            pltpu.VMEM((4 * CAP, R), jnp.bfloat16),
            pltpu.SemaphoreType.DMA((4,)),
            pltpu.SemaphoreType.DMA((16,)),
        ],
        compiler_params=pltpu.CompilerParams(vmem_limit_bytes=24 << 20),
        name="update",
    )(*rows, *chunks)


def apply_kernel(d, value, weight, *refs):
    out, new_weight, rows, weights, in_sems, out_sems = refs[-6:]
    expert = lax.rem(places()[3] + d, 4)
    parts = [slice(at, at + R // 4) for at in range(0, R, R // 4)]
    loads = [
        pltpu.make_async_copy(weight.at[expert, :, part], weights.at[:, part], in_sems.at[i])
        for i, part in enumerate(parts)
    ]
    for load in loads:
        load.start()
    stores = [pltpu.make_async_copy(value, out.at[expert], out_sems.at[4])]
    stores[0].start()
    for i, part in enumerate(parts):
        loads[i].wait()
        rows[:, part] = (
            weights[:, part] * (1.0 - learn_rate * decay_rate)
            - learn_rate * value[:, part].astype(jnp.float32)
        )
        stores.append(pltpu.make_async_copy(
            rows.at[:, part], new_weight.at[expert, :, part], out_sems.at[i]
        ))
        stores[-1].start()
    for store in stores:
        store.wait()


def apply(d, value, weight, outs):
    anywhere = pl.BlockSpec(memory_space=pltpu.HBM)
    return pl.pallas_call(
        functools.partial(apply_kernel, d),
        out_shape=[
            jax.ShapeDtypeStruct((4, CAP, R), jnp.bfloat16),
            jax.ShapeDtypeStruct((4, CAP, R), jnp.float32),
        ],
        in_specs=[pl.BlockSpec(memory_space=pltpu.VMEM), anywhere] + [anywhere] * len(outs),
        out_specs=[anywhere, anywhere],
        scratch_shapes=[
            pltpu.VMEM((CAP, R), jnp.float32),
            pltpu.VMEM((CAP, R), jnp.float32),
            pltpu.SemaphoreType.DMA((4,)),
            pltpu.SemaphoreType.DMA((5,)),
        ],
        input_output_aliases={2: 0, 3: 1} if outs else {},
        compiler_params=pltpu.CompilerParams(vmem_limit_bytes=8 << 20),
        cost_estimate=pl.CostEstimate(flops=CAP * R * 3, bytes_accessed=CAP * R * 12, transcendentals=0),
        name="apply",
    )(value, weight, *outs)


def summed(parts):
    total = None
    for part in parts:
        part = part.astype(jnp.float32)
        total = part if total is None else total + part
    return total.astype(jnp.bfloat16)


def on_device(momentum, lengths, weight):
    routes = {d: to_expert(d) for d in (1, 2, 3)}
    rows = live(lengths.reshape(1, 4), momentum)
    rows = [rows[0]] + [shift(rows[d], routes[d]) for d in (1, 2, 3)]
    other_rows = [shift(part, OTHER_CORE) for part in rows]

    total = gram([rows[0]])
    total = gram(rows[1:], total, weight=40)
    parts = gram(other_rows, total, last=True)
    rings = (RING_P, RING_Q)
    chunks = []
    for route in range(2):
        mine = parts[route * 4:route * 4 + 4]
        chunks.append([mine[0]] + [shift(mine[k], rings[route][k]) for k in (2, 1, 3)])
    chunks = [summed(got) for got in chunks]
    chunks = [
        [chunks[route]] + [shift(chunks[route], rings[1 - route][k]) for k in (2, 1, 3)]
        for route in range(2)
    ]
    chunks = [summed(got) for got in chunks]
    mine, others = [], []
    for route in range(2):
        got = [chunks[route]] + [shift(chunks[route], rings[route][k]) for k in (1, 2, 3)]
        mine += got
        others += [
            shift(part, OTHER_CORE)
            for part in (jnp.concatenate([got[0], got[3]], 0), got[2], got[1])
        ]

    updates = update(rows, mine + others)
    outs = apply(0, updates[0], weight, [])
    for d in (1, 2, 3):
        outs = apply(d, shift(updates[d], flipped(routes[d])), weight, outs)
    return tuple(outs)


def solution(mesh):
    placed = (
        P(None, ("group", "col"), None),
        P(None, ("group", "col")),
        P(None, ("group", "col"), None),
    )
    return jax.shard_map(
        on_device,
        mesh=mesh,
        in_specs=placed,
        out_specs=(P(None, ("group", "col"), None), P(None, ("group", "col"), None)),
        check_vma=False,
    )
```

```python
import functools
import math

import jax
import jax.numpy as jnp
from jax import lax
from jax.experimental import pallas as pl
from jax.experimental.pallas import tpu as pltpu
from jax.sharding import PartitionSpec as P

C = 7168
R = 2048
CAP = 112
AXES = ("group", "col")
OFFSETS = (0, 2, 1, 3)

quintic_first = 3.4445
quintic_second = -4.775
quintic_third = 2.0315
margin_square = 2.25
epsilon_norm = 1e-06
learn_rate = 0.02
decay_rate = 0.1

BLOCK = 256
HALF_BLOCK = BLOCK // 2
SAME = [(a, b) for a in range(4) for b in range(a + 1, 4)]
OFF = 14
SLOTS = OFF + 4
TOPS = OFF * BLOCK
CORNERS = TOPS + 4 * HALF_BLOCK
HALF = CORNERS + 2 * HALF_BLOCK
ROUTE = HALF // 2
CHUNK = ROUTE // 4


def pairs(move):
    def place(x, y, z, c):
        return (x % 4) * 32 + (y % 4) * 8 + (z % 4) * 2 + c

    return [
        (place(x, y, z, c), place(*move(x, y, z, c)))
        for x in range(4) for y in range(4) for z in range(4) for c in range(2)
    ]


def flipped(steps):
    return [(b, a) for a, b in steps]


def to_expert(d):
    def move(x, y, z, c):
        along_x = (c == 0) != (d == 2)
        return (x + d, y, z, c) if along_x else (x, y + d, z, c)

    return pairs(move)


RING_P = {k: pairs(lambda x, y, z, c, k=k: (x + k, y - k, z, c)) for k in (1, 2, 3)}
RING_Q = {k: pairs(lambda x, y, z, c, k=k: (x, y, z + k, c)) for k in (1, 2, 3)}
OTHER_CORE = pairs(lambda x, y, z, c: (x, y, z, 1 - c))


def shift(value, steps):
    return lax.ppermute(value, AXES, steps)


def places():
    x, col = lax.axis_index("group"), lax.axis_index("col")
    return col % 2, x, col // 2 % 4, (x + col // 8) % 4


def live_kernel(lengths, momentum, o0, o1, o2, o3, rows, sems):
    home = places()[3]
    outs = (o0, o1, o2, o3)
    experts = [lax.rem(home + d, 4) for d in OFFSETS]
    loads = [
        pltpu.make_async_copy(momentum.at[experts[d]], rows.at[d], sems.at[d])
        for d in range(4)
    ]
    for load in loads:
        load.start()
    lane = lax.broadcasted_iota(jnp.int32, (1, 4), 1)
    for d in (1, 2, 3, 0):
        loads[d].wait()
        slot = lax.broadcasted_iota(jnp.int32, (CAP, 128), 0)
        keep = slot < jnp.sum(jnp.where(lane == experts[d], lengths[...], 0))
        keep = jnp.where(keep, 1.0, 0.0).astype(jnp.bfloat16)
        for at in range(0, R, 128):
            value = rows[d, :, at:at + 128]
            outs[d][:, at:at + 128] = value * keep


def live(lengths, momentum):
    return pl.pallas_call(
        live_kernel,
        out_shape=[jax.ShapeDtypeStruct((CAP, R), jnp.bfloat16)] * 4,
        in_specs=[
            pl.BlockSpec(memory_space=pltpu.VMEM),
            pl.BlockSpec(memory_space=pltpu.HBM),
        ],
        out_specs=[pl.BlockSpec(memory_space=pltpu.VMEM)] * 4,
        scratch_shapes=[
            pltpu.VMEM((4, CAP, R), jnp.bfloat16),
            pltpu.SemaphoreType.DMA((4,)),
        ],
        compiler_params=pltpu.CompilerParams(vmem_limit_bytes=61 << 20),
        name="live",
    )(lengths, momentum)


def gram_kernel(count, first_stage, last_stage, *refs):
    rows, rest = refs[:count], refs[count:]
    if not first_stage:
        before, rest = rest[0], rest[1:]
    if last_stage:
        outs, rest = rest[:8], rest[8:]
        blocks, out_sems = rest[-2:]
    else:
        total, rest = rest[0], rest[1:]
    x_all, x_turned, in_sems = rest[:3]
    core, p, q, _ = places()
    loads = [
        pltpu.make_async_copy(rows[i], x_all.at[pl.ds(CAP * i, CAP)], in_sems.at[i])
        for i in range(count)
    ]
    for load in loads:
        load.start()
    for load in loads:
        load.wait()

    def columns(at):
        return pl.ds(pl.multiple_of(at * BLOCK, BLOCK), BLOCK)

    for a in range(4):
        x_turned[a * BLOCK:(a + 1) * BLOCK, :] = x_all[:, columns(core * 4 + a)].T
    for slot in range(SLOTS):
        a, b = SAME[slot] if slot < 6 else (slot - OFF, slot - OFF)
        at = core * 4 + b
        if 6 <= slot < OFF:
            s = slot - 6
            a = jnp.where(core == 0, s // 2, 2 + s // 4)
            at = jnp.where(core == 0, 4 + s % 2, s % 4)
        value = jnp.dot(
            x_turned[columns(a), :], x_all[:, columns(at)], preferred_element_type=jnp.float32
        )
        here = slice(slot * BLOCK, (slot + 1) * BLOCK)
        if not first_stage:
            value = value + before[here, :]
        if not last_stage:
            total[here, :] = value
            continue
        value = value.astype(jnp.bfloat16)
        if slot < OFF:
            blocks[here, :] = value
        else:
            top = TOPS + a * HALF_BLOCK
            blocks[top:top + HALF_BLOCK, :] = value[:HALF_BLOCK]
            corner, side = CORNERS + a // 2 * HALF_BLOCK, a % 2 * HALF_BLOCK
            blocks[corner:corner + HALF_BLOCK, side:side + HALF_BLOCK] = value[HALF_BLOCK:, HALF_BLOCK:]
    if not last_stage:
        return
    stores = []
    for route, own in ((0, p), (1, q)):
        for k in range(4):
            start = route * ROUTE + lax.rem(own + k, 4) * CHUNK
            stores.append(pltpu.make_async_copy(
                blocks.at[pl.ds(pl.multiple_of(start, 16), CHUNK)],
                outs[route * 4 + k],
                out_sems.at[route * 4 + k],
            ))
    for store in stores:
        store.start()
    for store in stores:
        store.wait()


def gram(rows, before=None, last=False, weight=1):
    count, depth = len(rows), len(rows) * CAP
    vmem = pl.BlockSpec(memory_space=pltpu.VMEM)
    anywhere = pl.BlockSpec(memory_space=pl.ANY)
    scratch = [
        pltpu.VMEM((depth, R), jnp.bfloat16),
        pltpu.VMEM((4 * BLOCK, depth), jnp.bfloat16),
        pltpu.SemaphoreType.DMA((count,)),
    ]
    if last:
        out_shape = [jax.ShapeDtypeStruct((CHUNK, BLOCK), jnp.bfloat16)] * 8
        scratch += [pltpu.VMEM((HALF, BLOCK), jnp.bfloat16), pltpu.SemaphoreType.DMA((8,))]
    else:
        out_shape = jax.ShapeDtypeStruct((SLOTS * BLOCK, BLOCK), jnp.float32)
    operands = list(rows) + ([] if before is None else [before])
    return pl.pallas_call(
        functools.partial(gram_kernel, count, before is None, last),
        out_shape=out_shape,
        in_specs=[anywhere] * count + [vmem] * (before is not None),
        out_specs=[anywhere] * 8 if last else vmem,
        scratch_shapes=scratch,
        input_output_aliases={count: 0} if before is not None and not last else {},
        compiler_params=pltpu.CompilerParams(vmem_limit_bytes=16 << 20),
        cost_estimate=pl.CostEstimate(
            flops=2 * SLOTS * BLOCK * BLOCK * depth * weight,
            bytes_accessed=depth * R * 2 + 2 * SLOTS * BLOCK * BLOCK * 4,
            transcendentals=0,
        ),
        name="gram",
    )(*operands)


def stored_at(i, j):
    if i // 4 == j // 4:
        a, b = i % 4, j % 4
        return i // 4, SAME.index((min(a, b), max(a, b))), a > b
    low, high = min(i, j), max(i, j)
    if high < 6:
        return 0, 6 + 2 * low + (high - 4), i > j
    return 1, 6 + 4 * (high - 6) + low, i < j


def update_kernel(*refs):
    rows, chunks, outs = refs[:4], refs[4:18], refs[18:22]
    x_all, blocks, diagonal, first, first_round, in_sems, chunk_sems = refs[22:]
    core, p, q, _ = places()
    loads = [
        pltpu.make_async_copy(rows[i], x_all.at[pl.ds(CAP * i, CAP)], in_sems.at[i])
        for i in range(4)
    ]
    for side in range(2):
        half = core if side == 0 else 1 - core
        for route, own in ((0, p), (1, q)):
            for k in range(4):
                if side == 0:
                    chunk = chunks[route * 4 + k]
                elif k in (0, 2):
                    chunk = chunks[8 + route * 3].at[pl.ds(k // 2 * CHUNK, CHUNK)]
                else:
                    chunk = chunks[8 + route * 3 + 2 - k // 3]
                number = half * 8 + route * 4 + lax.rem(own + 4 - k, 4)
                loads.append(pltpu.make_async_copy(
                    chunk,
                    blocks.at[pl.ds(pl.multiple_of(number * CHUNK, 16), CHUNK)],
                    chunk_sems.at[number],
                ))
    for load in loads:
        load.start()

    def block(half, slot):
        start = half * HALF + slot * BLOCK
        return blocks[start:start + BLOCK, :]

    def times_gram(left, j):
        total = None
        for i in range(8):
            if i == j:
                part, turned = diagonal[j * BLOCK:(j + 1) * BLOCK, :], False
            else:
                half, slot, turned = stored_at(i, j)
                part = block(half, slot)
            term = lax.dot_general(
                left[:, i * BLOCK:(i + 1) * BLOCK],
                part,
                (((1,), (1 if turned else 0,)), ((), ())),
                preferred_element_type=jnp.float32,
            )
            total = term if total is None else total + term
        return total

    def squared(value):
        value = value.astype(jnp.float32)
        return value * value

    for number in range(16):
        here = blocks.at[pl.ds(number * CHUNK, CHUNK)]
        pltpu.make_async_copy(here, here, chunk_sems.at[number]).wait()
    twice = jnp.zeros((16, BLOCK), jnp.float32)
    once = jnp.zeros((HALF_BLOCK, HALF_BLOCK), jnp.float32)
    for i in range(8):
        half, a = i // 4, i % 4
        start = half * HALF + TOPS + a * HALF_BLOCK
        corner, side = half * HALF + CORNERS + a // 2 * HALF_BLOCK, a % 2 * HALF_BLOCK
        top = blocks[start:start + HALF_BLOCK, :]
        last = blocks[corner:corner + HALF_BLOCK, side:side + HALF_BLOCK]
        diagonal[i * BLOCK:i * BLOCK + HALF_BLOCK, :] = top
        diagonal[i * BLOCK + HALF_BLOCK:(i + 1) * BLOCK, :HALF_BLOCK] = top[:, HALF_BLOCK:].T
        diagonal[i * BLOCK + HALF_BLOCK:(i + 1) * BLOCK, HALF_BLOCK:] = last
        once += squared(top[:, :HALF_BLOCK]) + squared(last) + 2.0 * squared(top[:, HALF_BLOCK:])
    for load in loads[:4]:
        load.wait()

    for j in range(8):
        at = slice(j * BLOCK, (j + 1) * BLOCK)
        value = times_gram(x_all, j)
        first[:, at] = value
        first_round[:, at] = value.astype(jnp.bfloat16)
        for at in range(2 * j * CHUNK, 2 * (j + 1) * CHUNK, 16):
            if at % HALF < TOPS:
                twice += squared(blocks[at:at + 16, :])
    total = 2.0 * jnp.sum(twice, axis=(0, 1), keepdims=True) + jnp.sum(once, axis=(0, 1), keepdims=True)
    norm_scale = margin_square / (jnp.sqrt(total) + epsilon_norm)
    root = jnp.sqrt(norm_scale)
    for j in range(8):
        at = slice(j * BLOCK, (j + 1) * BLOCK)
        second = times_gram(first_round, j)
        scaled = (x_all[:, at].astype(jnp.float32) * root).astype(jnp.bfloat16)
        combined = (
            quintic_first * scaled.astype(jnp.float32)
            + (quintic_second * norm_scale * root) * first[:, at]
            + (quintic_third * norm_scale * norm_scale * root) * second
        )
        value = (math.sqrt(C) * combined).astype(jnp.bfloat16)
        for d in range(4):
            outs[d][:, at] = value[CAP * d:CAP * (d + 1)]


def update(rows, chunks):
    anywhere = pl.BlockSpec(memory_space=pl.ANY)
    return pl.pallas_call(
        update_kernel,
        out_shape=[jax.ShapeDtypeStruct((CAP, R), jnp.bfloat16)] * 4,
        in_specs=[anywhere] * 18,
        out_specs=[pl.BlockSpec(memory_space=pltpu.VMEM)] * 4,
        scratch_shapes=[
            pltpu.VMEM((4 * CAP, R), jnp.bfloat16),
            pltpu.VMEM((2 * HALF, BLOCK), jnp.bfloat16),
            pltpu.VMEM((R, BLOCK), jnp.bfloat16),
            pltpu.VMEM((4 * CAP, R), jnp.float32),
            pltpu.VMEM((4 * CAP, R), jnp.bfloat16),
            pltpu.SemaphoreType.DMA((4,)),
            pltpu.SemaphoreType.DMA((16,)),
        ],
        compiler_params=pltpu.CompilerParams(vmem_limit_bytes=24 << 20),
        name="update",
    )(*rows, *chunks)


def apply_kernel(d, value, weight, *refs):
    out, new_weight, rows, weights, in_sems, out_sems = refs[-6:]
    expert = lax.rem(places()[3] + OFFSETS[d], 4)
    parts = [slice(at, at + R // 4) for at in range(0, R, R // 4)]
    loads = [
        pltpu.make_async_copy(weight.at[expert, :, part], weights.at[:, part], in_sems.at[i])
        for i, part in enumerate(parts)
    ]
    for load in loads:
        load.start()
    stores = [pltpu.make_async_copy(value, out.at[expert], out_sems.at[4])]
    stores[0].start()
    for i, part in enumerate(parts):
        loads[i].wait()
        rows[:, part] = (
            weights[:, part] * (1.0 - learn_rate * decay_rate)
            - learn_rate * value[:, part].astype(jnp.float32)
        )
        stores.append(pltpu.make_async_copy(
            rows.at[:, part], new_weight.at[expert, :, part], out_sems.at[i]
        ))
        stores[-1].start()
    for store in stores:
        store.wait()


def apply(d, value, weight, outs):
    anywhere = pl.BlockSpec(memory_space=pltpu.HBM)
    return pl.pallas_call(
        functools.partial(apply_kernel, d),
        out_shape=[
            jax.ShapeDtypeStruct((4, CAP, R), jnp.bfloat16),
            jax.ShapeDtypeStruct((4, CAP, R), jnp.float32),
        ],
        in_specs=[pl.BlockSpec(memory_space=pltpu.VMEM), anywhere] + [anywhere] * len(outs),
        out_specs=[anywhere, anywhere],
        scratch_shapes=[
            pltpu.VMEM((CAP, R), jnp.float32),
            pltpu.VMEM((CAP, R), jnp.float32),
            pltpu.SemaphoreType.DMA((4,)),
            pltpu.SemaphoreType.DMA((5,)),
        ],
        input_output_aliases={2: 0, 3: 1} if outs else {},
        compiler_params=pltpu.CompilerParams(vmem_limit_bytes=8 << 20),
        cost_estimate=pl.CostEstimate(flops=CAP * R * 3, bytes_accessed=CAP * R * 12, transcendentals=0),
        name="apply",
    )(value, weight, *outs)


def summed(parts):
    total = None
    for part in parts:
        part = part.astype(jnp.float32)
        total = part if total is None else total + part
    return total.astype(jnp.bfloat16)


def on_device(momentum, lengths, weight):
    routes = {d: to_expert(OFFSETS[d]) for d in (1, 2, 3)}
    rows = live(lengths.reshape(1, 4), momentum)
    rows = [rows[0]] + [shift(rows[d], routes[d]) for d in (1, 2, 3)]
    other_rows = [shift(part, OTHER_CORE) for part in rows]

    total = gram([rows[0]])
    total = gram(rows[1:], total, weight=40)
    parts = gram(other_rows, total, last=True)
    rings = (RING_P, RING_Q)
    chunks = []
    for route in range(2):
        mine = parts[route * 4:route * 4 + 4]
        chunks.append([mine[0]] + [shift(mine[k], rings[route][k]) for k in (2, 1, 3)])
    chunks = [summed(got) for got in chunks]
    chunks = [
        [chunks[route]] + [shift(chunks[route], rings[1 - route][k]) for k in (2, 1, 3)]
        for route in range(2)
    ]
    chunks = [summed(got) for got in chunks]
    mine, others = [], []
    for route in range(2):
        got = [chunks[route]] + [shift(chunks[route], rings[route][k]) for k in (1, 2, 3)]
        mine += got
        others += [
            shift(part, OTHER_CORE)
            for part in (jnp.concatenate([got[0], got[2]], 0), got[3], got[1])
        ]

    updates = update(rows, mine + others)
    outs = apply(0, updates[0], weight, [])
    for d in (1, 2, 3):
        outs = apply(d, shift(updates[d], flipped(routes[d])), weight, outs)
    return tuple(outs)


def solution(mesh):
    placed = (
        P(None, ("group", "col"), None),
        P(None, ("group", "col")),
        P(None, ("group", "col"), None),
    )
    return jax.shard_map(
        on_device,
        mesh=mesh,
        in_specs=placed,
        out_specs=(P(None, ("group", "col"), None), P(None, ("group", "col"), None)),
        check_vma=False,
    )
```

```python
import functools
import math

import jax
import jax.numpy as jnp
from jax import lax
from jax.experimental import pallas as pl
from jax.experimental.pallas import tpu as pltpu
from jax.sharding import PartitionSpec as P

C = 7168
R = 2048
CAP = 112
AXES = ("group", "col")
OFFSETS = (0, 2, 1, 3)

quintic_first = 3.4445
quintic_second = -4.775
quintic_third = 2.0315
margin_square = 2.25
epsilon_norm = 1e-06
learn_rate = 0.02
decay_rate = 0.1

BLOCK = 256
HALF_BLOCK = BLOCK // 2
SAME = [(a, b) for a in range(4) for b in range(a + 1, 4)]
OFF = 14
SLOTS = OFF + 4
TOPS = OFF * BLOCK
CORNERS = TOPS + 4 * HALF_BLOCK
HALF = CORNERS + 2 * HALF_BLOCK
ROUTE = HALF // 2
CHUNK = ROUTE // 4


def pairs(move):
    def place(x, y, z, c):
        return (x % 4) * 32 + (y % 4) * 8 + (z % 4) * 2 + c

    return [
        (place(x, y, z, c), place(*move(x, y, z, c)))
        for x in range(4) for y in range(4) for z in range(4) for c in range(2)
    ]


def flipped(steps):
    return [(b, a) for a, b in steps]


def to_expert(d):
    def move(x, y, z, c):
        along_x = (c == 0) != (d == 2)
        return (x + d, y, z, c) if along_x else (x, y + d, z, c)

    return pairs(move)


RING_P = {k: pairs(lambda x, y, z, c, k=k: (x + k, y - k, z, c)) for k in (1, 2, 3)}
RING_Q = {k: pairs(lambda x, y, z, c, k=k: (x, y, z + k, c)) for k in (1, 2, 3)}
OTHER_CORE = pairs(lambda x, y, z, c: (x, y, z, 1 - c))


def shift(value, steps):
    return lax.ppermute(value, AXES, steps)


def places():
    x, col = lax.axis_index("group"), lax.axis_index("col")
    return col % 2, x, col // 2 % 4, (x + col // 8) % 4


def live_kernel(which, lengths, momentum, *refs):
    home = places()[3]
    outs, (rows, sems) = refs[:-2], refs[-2:]
    experts = [lax.rem(home + OFFSETS[i], 4) for i in which]
    loads = [
        pltpu.make_async_copy(momentum.at[experts[d]], rows.at[d], sems.at[d])
        for d in range(len(which))
    ]
    for load in loads:
        load.start()
    lane = lax.broadcasted_iota(jnp.int32, (1, 4), 1)
    for d in range(len(which)):
        loads[d].wait()
        slot = lax.broadcasted_iota(jnp.int32, (CAP, 128), 0)
        keep = slot < jnp.sum(jnp.where(lane == experts[d], lengths[...], 0))
        keep = jnp.where(keep, 1.0, 0.0).astype(jnp.bfloat16)
        for at in range(0, R, 128):
            value = rows[d, :, at:at + 128]
            outs[d][:, at:at + 128] = value * keep


def live(which, lengths, momentum):
    return pl.pallas_call(
        functools.partial(live_kernel, which),
        out_shape=[jax.ShapeDtypeStruct((CAP, R), jnp.bfloat16)] * len(which),
        in_specs=[
            pl.BlockSpec(memory_space=pltpu.VMEM),
            pl.BlockSpec(memory_space=pltpu.HBM),
        ],
        out_specs=[pl.BlockSpec(memory_space=pltpu.VMEM)] * len(which),
        scratch_shapes=[
            pltpu.VMEM((len(which), CAP, R), jnp.bfloat16),
            pltpu.SemaphoreType.DMA((len(which),)),
        ],
        compiler_params=pltpu.CompilerParams(vmem_limit_bytes=(61 if len(which) == 1 else 16) << 20),
        name="live",
    )(lengths, momentum)


def gram_kernel(count, first_stage, last_stage, *refs):
    rows, rest = refs[:count], refs[count:]
    if not first_stage:
        before, rest = rest[0], rest[1:]
    if last_stage:
        outs, rest = rest[:8], rest[8:]
        blocks, out_sems = rest[-2:]
    else:
        total, rest = rest[0], rest[1:]
    x_all, x_turned, in_sems = rest[:3]
    core, p, q, _ = places()
    loads = [
        pltpu.make_async_copy(rows[i], x_all.at[pl.ds(CAP * i, CAP)], in_sems.at[i])
        for i in range(count)
    ]
    for load in loads:
        load.start()
    for load in loads:
        load.wait()

    def columns(at):
        return pl.ds(pl.multiple_of(at * BLOCK, BLOCK), BLOCK)

    for a in range(4):
        x_turned[a * BLOCK:(a + 1) * BLOCK, :] = x_all[:, columns(core * 4 + a)].T
    for slot in range(SLOTS):
        a, b = SAME[slot] if slot < 6 else (slot - OFF, slot - OFF)
        at = core * 4 + b
        if 6 <= slot < OFF:
            s = slot - 6
            a = jnp.where(core == 0, s // 2, 2 + s // 4)
            at = jnp.where(core == 0, 4 + s % 2, s % 4)
        value = jnp.dot(
            x_turned[columns(a), :], x_all[:, columns(at)], preferred_element_type=jnp.float32
        )
        here = slice(slot * BLOCK, (slot + 1) * BLOCK)
        if not first_stage:
            value = value + before[here, :]
        if not last_stage:
            total[here, :] = value
            continue
        value = value.astype(jnp.bfloat16)
        if slot < OFF:
            blocks[here, :] = value
        else:
            top = TOPS + a * HALF_BLOCK
            blocks[top:top + HALF_BLOCK, :] = value[:HALF_BLOCK]
            corner, side = CORNERS + a // 2 * HALF_BLOCK, a % 2 * HALF_BLOCK
            blocks[corner:corner + HALF_BLOCK, side:side + HALF_BLOCK] = value[HALF_BLOCK:, HALF_BLOCK:]
    if not last_stage:
        return
    stores = []
    for route, own in ((0, p), (1, q)):
        for k in range(4):
            start = route * ROUTE + lax.rem(own + k, 4) * CHUNK
            stores.append(pltpu.make_async_copy(
                blocks.at[pl.ds(pl.multiple_of(start, 16), CHUNK)],
                outs[route * 4 + k],
                out_sems.at[route * 4 + k],
            ))
    for store in stores:
        store.start()
    for store in stores:
        store.wait()


def gram(rows, before=None, last=False, weight=1):
    count, depth = len(rows), len(rows) * CAP
    vmem = pl.BlockSpec(memory_space=pltpu.VMEM)
    anywhere = pl.BlockSpec(memory_space=pl.ANY)
    scratch = [
        pltpu.VMEM((depth, R), jnp.bfloat16),
        pltpu.VMEM((4 * BLOCK, depth), jnp.bfloat16),
        pltpu.SemaphoreType.DMA((count,)),
    ]
    if last:
        out_shape = [jax.ShapeDtypeStruct((CHUNK, BLOCK), jnp.bfloat16)] * 8
        scratch += [pltpu.VMEM((HALF, BLOCK), jnp.bfloat16), pltpu.SemaphoreType.DMA((8,))]
    else:
        out_shape = jax.ShapeDtypeStruct((SLOTS * BLOCK, BLOCK), jnp.float32)
    operands = list(rows) + ([] if before is None else [before])
    return pl.pallas_call(
        functools.partial(gram_kernel, count, before is None, last),
        out_shape=out_shape,
        in_specs=[anywhere] * count + [vmem] * (before is not None),
        out_specs=[anywhere] * 8 if last else vmem,
        scratch_shapes=scratch,
        input_output_aliases={count: 0} if before is not None and not last else {},
        compiler_params=pltpu.CompilerParams(vmem_limit_bytes=16 << 20),
        cost_estimate=pl.CostEstimate(
            flops=2 * SLOTS * BLOCK * BLOCK * depth * weight,
            bytes_accessed=depth * R * 2 + 2 * SLOTS * BLOCK * BLOCK * 4,
            transcendentals=0,
        ),
        name="gram",
    )(*operands)


def stored_at(i, j):
    if i // 4 == j // 4:
        a, b = i % 4, j % 4
        return i // 4, SAME.index((min(a, b), max(a, b))), a > b
    low, high = min(i, j), max(i, j)
    if high < 6:
        return 0, 6 + 2 * low + (high - 4), i > j
    return 1, 6 + 4 * (high - 6) + low, i < j


def update_kernel(*refs):
    rows, chunks, outs = refs[:4], refs[4:18], refs[18:22]
    x_all, blocks, diagonal, first, first_round, in_sems, chunk_sems = refs[22:]
    core, p, q, _ = places()
    loads = [
        pltpu.make_async_copy(rows[i], x_all.at[pl.ds(CAP * i, CAP)], in_sems.at[i])
        for i in range(4)
    ]
    for side in range(2):
        half = core if side == 0 else 1 - core
        for route, own in ((0, p), (1, q)):
            for k in range(4):
                if side == 0:
                    chunk = chunks[route * 4 + k]
                elif k in (0, 2):
                    chunk = chunks[8 + route * 3].at[pl.ds(k // 2 * CHUNK, CHUNK)]
                else:
                    chunk = chunks[8 + route * 3 + 2 - k // 3]
                number = half * 8 + route * 4 + lax.rem(own + 4 - k, 4)
                loads.append(pltpu.make_async_copy(
                    chunk,
                    blocks.at[pl.ds(pl.multiple_of(number * CHUNK, 16), CHUNK)],
                    chunk_sems.at[number],
                ))
    for load in loads:
        load.start()

    def block(half, slot):
        start = half * HALF + slot * BLOCK
        return blocks[start:start + BLOCK, :]

    def times_gram(left, j):
        total = None
        for i in range(8):
            if i == j:
                part, turned = diagonal[j * BLOCK:(j + 1) * BLOCK, :], False
            else:
                half, slot, turned = stored_at(i, j)
                part = block(half, slot)
            term = lax.dot_general(
                left[:, i * BLOCK:(i + 1) * BLOCK],
                part,
                (((1,), (1 if turned else 0,)), ((), ())),
                preferred_element_type=jnp.float32,
            )
            total = term if total is None else total + term
        return total

    def squared(value):
        value = value.astype(jnp.float32)
        return value * value

    for number in range(16):
        here = blocks.at[pl.ds(number * CHUNK, CHUNK)]
        pltpu.make_async_copy(here, here, chunk_sems.at[number]).wait()
    twice = jnp.zeros((16, BLOCK), jnp.float32)
    once = jnp.zeros((HALF_BLOCK, HALF_BLOCK), jnp.float32)
    for i in range(8):
        half, a = i // 4, i % 4
        start = half * HALF + TOPS + a * HALF_BLOCK
        corner, side = half * HALF + CORNERS + a // 2 * HALF_BLOCK, a % 2 * HALF_BLOCK
        top = blocks[start:start + HALF_BLOCK, :]
        last = blocks[corner:corner + HALF_BLOCK, side:side + HALF_BLOCK]
        diagonal[i * BLOCK:i * BLOCK + HALF_BLOCK, :] = top
        diagonal[i * BLOCK + HALF_BLOCK:(i + 1) * BLOCK, :HALF_BLOCK] = top[:, HALF_BLOCK:].T
        diagonal[i * BLOCK + HALF_BLOCK:(i + 1) * BLOCK, HALF_BLOCK:] = last
        once += squared(top[:, :HALF_BLOCK]) + squared(last) + 2.0 * squared(top[:, HALF_BLOCK:])
    for load in loads[:4]:
        load.wait()

    for j in range(8):
        at = slice(j * BLOCK, (j + 1) * BLOCK)
        value = times_gram(x_all, j)
        first[:, at] = value
        first_round[:, at] = value.astype(jnp.bfloat16)
        for at in range(2 * j * CHUNK, 2 * (j + 1) * CHUNK, 16):
            if at % HALF < TOPS:
                twice += squared(blocks[at:at + 16, :])
    total = 2.0 * jnp.sum(twice, axis=(0, 1), keepdims=True) + jnp.sum(once, axis=(0, 1), keepdims=True)
    norm_scale = margin_square / (jnp.sqrt(total) + epsilon_norm)
    root = jnp.sqrt(norm_scale)
    for j in range(8):
        at = slice(j * BLOCK, (j + 1) * BLOCK)
        second = times_gram(first_round, j)
        scaled = (x_all[:, at].astype(jnp.float32) * root).astype(jnp.bfloat16)
        combined = (
            quintic_first * scaled.astype(jnp.float32)
            + (quintic_second * norm_scale * root) * first[:, at]
            + (quintic_third * norm_scale * norm_scale * root) * second
        )
        value = (math.sqrt(C) * combined).astype(jnp.bfloat16)
        for d in range(4):
            outs[d][:, at] = value[CAP * d:CAP * (d + 1)]


def update(rows, chunks):
    anywhere = pl.BlockSpec(memory_space=pl.ANY)
    return pl.pallas_call(
        update_kernel,
        out_shape=[jax.ShapeDtypeStruct((CAP, R), jnp.bfloat16)] * 4,
        in_specs=[anywhere] * 18,
        out_specs=[pl.BlockSpec(memory_space=pltpu.VMEM)] * 4,
        scratch_shapes=[
            pltpu.VMEM((4 * CAP, R), jnp.bfloat16),
            pltpu.VMEM((2 * HALF, BLOCK), jnp.bfloat16),
            pltpu.VMEM((R, BLOCK), jnp.bfloat16),
            pltpu.VMEM((4 * CAP, R), jnp.float32),
            pltpu.VMEM((4 * CAP, R), jnp.bfloat16),
            pltpu.SemaphoreType.DMA((4,)),
            pltpu.SemaphoreType.DMA((16,)),
        ],
        compiler_params=pltpu.CompilerParams(vmem_limit_bytes=24 << 20),
        name="update",
    )(*rows, *chunks)


def apply_kernel(d, value, weight, *refs):
    out, new_weight, rows, weights, in_sems, out_sems = refs[-6:]
    expert = lax.rem(places()[3] + OFFSETS[d], 4)
    parts = [slice(at, at + R // 4) for at in range(0, R, R // 4)]
    loads = [
        pltpu.make_async_copy(weight.at[expert, :, part], weights.at[:, part], in_sems.at[i])
        for i, part in enumerate(parts)
    ]
    for load in loads:
        load.start()
    stores = [pltpu.make_async_copy(value, out.at[expert], out_sems.at[4])]
    stores[0].start()
    for i, part in enumerate(parts):
        loads[i].wait()
        rows[:, part] = (
            weights[:, part] * (1.0 - learn_rate * decay_rate)
            - learn_rate * value[:, part].astype(jnp.float32)
        )
        stores.append(pltpu.make_async_copy(
            rows.at[:, part], new_weight.at[expert, :, part], out_sems.at[i]
        ))
        stores[-1].start()
    for store in stores:
        store.wait()


def apply(d, value, weight, outs):
    anywhere = pl.BlockSpec(memory_space=pltpu.HBM)
    return pl.pallas_call(
        functools.partial(apply_kernel, d),
        out_shape=[
            jax.ShapeDtypeStruct((4, CAP, R), jnp.bfloat16),
            jax.ShapeDtypeStruct((4, CAP, R), jnp.float32),
        ],
        in_specs=[pl.BlockSpec(memory_space=pltpu.VMEM), anywhere] + [anywhere] * len(outs),
        out_specs=[anywhere, anywhere],
        scratch_shapes=[
            pltpu.VMEM((CAP, R), jnp.float32),
            pltpu.VMEM((CAP, R), jnp.float32),
            pltpu.SemaphoreType.DMA((4,)),
            pltpu.SemaphoreType.DMA((5,)),
        ],
        input_output_aliases={2: 0, 3: 1} if outs else {},
        compiler_params=pltpu.CompilerParams(vmem_limit_bytes=8 << 20),
        cost_estimate=pl.CostEstimate(flops=CAP * R * 3, bytes_accessed=CAP * R * 12, transcendentals=0),
        name="apply",
    )(value, weight, *outs)


def summed(parts):
    total = None
    for part in parts:
        part = part.astype(jnp.float32)
        total = part if total is None else total + part
    return total.astype(jnp.bfloat16)


def on_device(momentum, lengths, weight):
    routes = {d: to_expert(OFFSETS[d]) for d in (1, 2, 3)}
    (ahead,) = live((1,), lengths.reshape(1, 4), momentum)
    second, third, own = live((2, 3, 0), lengths.reshape(1, 4), momentum)
    rows = [own, ahead, second, third]
    rows = [rows[0]] + [shift(rows[d], routes[d]) for d in (1, 2, 3)]
    other_rows = [shift(part, OTHER_CORE) for part in rows]

    total = gram([rows[0]])
    total = gram(rows[1:], total, weight=40)
    parts = gram(other_rows, total, last=True)
    rings = (RING_P, RING_Q)
    chunks = []
    for route in range(2):
        mine = parts[route * 4:route * 4 + 4]
        chunks.append([mine[0]] + [shift(mine[k], rings[route][k]) for k in (2, 1, 3)])
    chunks = [summed(got) for got in chunks]
    chunks = [
        [chunks[route]] + [shift(chunks[route], rings[1 - route][k]) for k in (2, 1, 3)]
        for route in range(2)
    ]
    chunks = [summed(got) for got in chunks]
    mine, others = [], []
    for route in range(2):
        got = [chunks[route]] + [shift(chunks[route], rings[route][k]) for k in (1, 2, 3)]
        mine += got
        others += [
            shift(part, OTHER_CORE)
            for part in (jnp.concatenate([got[0], got[2]], 0), got[3], got[1])
        ]

    updates = update(rows, mine + others)
    outs = apply(0, updates[0], weight, [])
    for d in (1, 2, 3):
        outs = apply(d, shift(updates[d], flipped(routes[d])), weight, outs)
    return tuple(outs)


def solution(mesh):
    placed = (
        P(None, ("group", "col"), None),
        P(None, ("group", "col")),
        P(None, ("group", "col"), None),
    )
    return jax.shard_map(
        on_device,
        mesh=mesh,
        in_specs=placed,
        out_specs=(P(None, ("group", "col"), None), P(None, ("group", "col"), None)),
        check_vma=False,
    )
```
